512 devices in a mesh: member: 8 (over x, core), space: 64 (over z, y).
Axes of the slice: x: 4, y: 4, z: 16, core: 2. Of those that a mesh axis runs over, the one named last changes fastest.
Arguments:
- initial_state: float32 [8, 256, 256, 256], P('member', 'space'), may hold values from -6 to 6
- final_cotangent: float32 [8, 256, 256, 256], P('member', 'space'), may hold values from -6 to 6
- legendre: bfloat16 [256, 256, 256], P('space'), may hold values from -0.375 to 0.375
- wave_map: int32 [256], replicated, may hold values from 0 to 255, each once
- column_list: int32 [64, 2048], P('space'), may hold values from 0 to 2047, each once within a row
- column_count: int32 [64], P('space'), may hold values from 1 to 512, 16384 in all
- weight_in: bfloat16 [128, 384], replicated, may hold values from -0.5 to 0.5
- bias_in: float32 [384], replicated, may hold values from -3 to 3
- weight_out: bfloat16 [384, 128], replicated, may hold values from -0.3125 to 0.3125
- bias_out: float32 [128], replicated, may hold values from -3 to 3
Outputs:
- grad_state: float32 [8, 256, 256, 256], P('member', 'space')
- grad_weight_in: float32 [128, 384], replicated
- grad_bias_in: float32 [384], replicated
- grad_weight_out: float32 [384, 128], replicated
- grad_bias_out: float32 [128], replicated
The draws below stay inside these ranges and needn't reach their ends.
Inputs may be any that keep to these rules, and one draw needn't show every extreme that they name: Slot s of the spectral arrays and of legendre holds zonal wavenumber wave_map[s]; every wavenumber appears once. `column_list`: each row lists every local column of its band once; its first column_count entries are the band's active columns. `column_count`: the counts sum to 16384, and some band has exactly 512.
All inputs are finite; a program needn't handle non-finite values. No bound on the sum of `column_count` on one device may be relied on, other than what follows from the above.
Results may differ from the reference program's by a relative error of at most 0.0085.
Values may be sent and summed in bfloat16 or wider, within the bound.
No kernel may reach another device: no remote copies, remote signals or barrier semaphores. Data moves between devices by JAX's collectives and lax.ppermute only.
A program may use at most 64 MiB of HBM per device.

```python
import math
import jax
import jax.numpy as jnp
import numpy as np
from jax import lax

M = 256
J = 256
LAT = 256
LON = 512
F = 128
HID = 384
CAPA = 512
MEMBERS = 8
BANDS = 64
COLSD = 2048
ACTIVE = 16384


def levels(rng, extent, pieces, least, high):
    loudness, own = 1.0, jax.random.fold_in(rng, 6)
    for dim, shards_of in pieces:
        heights = jnp.exp(jax.random.uniform(jax.random.fold_in(own, dim), (shards_of,), jnp.float32, least / len(pieces), high / len(pieces)))
        loudness = loudness * jnp.repeat(heights, extent[dim] // shards_of).reshape([-1 if axis == dim else 1 for axis in range(len(extent))])
    return loudness


def length_profile(count, total, bound, skew):
    weights = [(1 << 20) // math.isqrt(standing ** skew) + 1 for standing in range(2, count + 1)]
    surplus, holding = total - bound - (count - 1), [1] * (count - 1)
    while surplus > 0:
        free = [i for i in range(count - 1) if holding[i] < bound]
        whole, budget = sum([weights[i] for i in free]), surplus
        for i in free:
            extra = min(bound - holding[i], max(1, budget * weights[i] // whole), surplus)
            holding[i] = holding[i] + extra
            surplus = surplus - extra
    return np.array([bound] + holding)


def uneven(key, amount, total, reach, skew):
    if amount == 2:
        one = jax.random.randint(key, (), max(1, total - reach), min(reach, total - 1) + 1)
        return jnp.stack([one, total - one])
    lengths = jnp.asarray(length_profile(amount, total, reach, skew), jnp.int32)
    pairs = (amount - 1) // 2
    giver, taker = lengths[1:1 + 2 * pairs:2], lengths[2:2 + 2 * pairs:2]
    margin = jnp.minimum(giver - 1, reach - taker)
    shifted = jax.random.randint(jax.random.fold_in(key, 1), (pairs,), 0, 1 << 20) % (margin + 1)
    lengths = lengths.at[1:1 + 2 * pairs:2].set(giver - shifted).at[2:2 + 2 * pairs:2].set(taker + shifted)
    return lengths[jax.random.permutation(jax.random.fold_in(key, 2), amount)]


def centred(rng, extent, scale, reach, cuts=(), kind=jnp.bfloat16):
    values = scale * jax.random.normal(rng, extent, jnp.float32)
    if cuts:
        values = values * levels(rng, extent, cuts, -0.22, 0.18)
    return jnp.clip(values, -reach, reach).astype(kind)


def setup_inputs(seed: int = 0) -> dict:
    arg_keys = jax.random.split(jax.random.key(seed), 11)
    return {
        "initial_state": centred(arg_keys[0], (MEMBERS, M, J, 2 * F), 1.0, 6.0, ((0, 8), (1, 64)), jnp.float32),
        "final_cotangent": centred(arg_keys[1], (MEMBERS, M, J, 2 * F), 1.0, 6.0, ((0, 8), (1, 64)), jnp.float32),
        "legendre": centred(arg_keys[2], (M, J, LAT), J ** -0.5, 0.375, ((0, 64),)),
        "wave_map": jax.random.permutation(arg_keys[3], M).astype(jnp.int32),
        "column_list": jax.vmap(lambda own: jax.random.permutation(own, COLSD))(jax.random.split(arg_keys[4], BANDS)).reshape((BANDS, COLSD)).astype(jnp.int32),
        "column_count": uneven(arg_keys[5], BANDS, ACTIVE, CAPA, 2).astype(jnp.int32),
        "weight_in": centred(arg_keys[6], (F, HID), F ** -0.5, 0.5),
        "bias_in": centred(arg_keys[7], (HID,), 0.5, 3.0, (), jnp.float32),
        "weight_out": centred(arg_keys[8], (HID, F), HID ** -0.5, 0.3125),
        "bias_out": centred(arg_keys[9], (F,), 0.5, 3.0, (), jnp.float32),
    }


step_size = 0.5

def fourier_table(wave_ids, lon_count, total_waves):
    longitude = jnp.arange(lon_count, dtype=jnp.int32)
    phase_index = wave_ids.astype(jnp.int32)[:, None] * longitude[None, :] % lon_count
    angles = phase_index.astype(jnp.float32) * (2.0 * math.pi / lon_count)
    norm_scale = 1.0 / math.sqrt(total_waves)
    stacked = jnp.stack([jnp.cos(angles), -jnp.sin(angles)], axis=1) * norm_scale
    return stacked.astype(jnp.bfloat16)

def spectral_factors(wave_ids, row_count, total_waves):
    degree = wave_ids.astype(jnp.int32)[:, None] + jnp.arange(row_count, dtype=jnp.int32)[None, :]
    truncation = (degree < total_waves).astype(jnp.float32)
    degree_real = degree.astype(jnp.float32)
    damping = 1.0 / (1.0 + degree_real * (degree_real + 1.0) / (total_waves * (total_waves - 1.0)))
    return (damping[:, :, None], truncation[:, :, None])

def synthesis(legendre, coeffs):
    return jnp.einsum('sjl,sjc->slc', legendre.astype(jnp.float32), coeffs.astype(jnp.float32))

def analysis(legendre, spectra):
    return jnp.einsum('sjl,slc->sjc', legendre.astype(jnp.float32), spectra.astype(jnp.float32))

def fourier_synthesis(wave_table, spectra):
    shaped = spectra.reshape(spectra.shape[0], spectra.shape[1], 2, -1)
    return jnp.einsum('slpf,spn->lnf', shaped.astype(jnp.float32), wave_table.astype(jnp.float32))

def fourier_analysis(wave_table, grid_all):
    result = jnp.einsum('lnf,spn->slpf', grid_all.astype(jnp.float32), wave_table.astype(jnp.float32))
    return result.reshape(result.shape[0], result.shape[1], -1)

def silu_slope(preact):
    sigmoid_val = jax.nn.sigmoid(preact)
    return sigmoid_val * (1.0 + preact * (1.0 - sigmoid_val))

def place_band(indices, values_band):
    return jnp.zeros((COLSD, values_band.shape[-1]), values_band.dtype).at[indices].set(values_band)

def reference(initial_state, final_cotangent, legendre, wave_map, column_list, column_count, weight_in, bias_in, weight_out, bias_out):
    wave_table = fourier_table(wave_map, LON, M)
    damping, truncation = spectral_factors(wave_map, J, M)
    index_list = column_list[:, :CAPA].astype(jnp.int32)
    valid_rows = (jnp.arange(CAPA, dtype=jnp.int32)[None, :] < column_count.astype(jnp.int32)[:, None]).astype(jnp.float32)[:, :, None]
    valid_half = valid_rows.astype(jnp.bfloat16)

    def gather_slots(grid_all):
        band_rows = grid_all.reshape(BANDS, COLSD, -1)
        return jnp.take_along_axis(band_rows, index_list[:, :, None], axis=1).reshape(BANDS * CAPA, -1)

    def place_slots(values_all, grid_shape):
        placed = jax.vmap(place_band)(index_list, values_all.reshape(BANDS, CAPA, -1))
        return placed.reshape(grid_shape)

    def physics_front(grid_all):
        inputs = gather_slots(grid_all)
        preact = jnp.dot(inputs, weight_in, preferred_element_type=jnp.float32) + bias_in
        active = jax.nn.silu(preact).astype(jnp.bfloat16)
        return (inputs, preact, active)

    def physics_tendency(active, grid_shape):
        output = jnp.dot(active, weight_out, preferred_element_type=jnp.float32) + bias_out
        output = (output.reshape(BANDS, CAPA, -1) * valid_rows).astype(jnp.bfloat16)
        return place_slots(output, grid_shape)

    def physics_adjoint(adjoint_grid, stored):
        inputs, preact, active = stored
        adjoint_out = (gather_slots(adjoint_grid).reshape(BANDS, CAPA, -1) * valid_half).reshape(BANDS * CAPA, -1)
        grad_w_out = jnp.dot(active.T, adjoint_out, preferred_element_type=jnp.float32)
        grad_b_out = lax.optimization_barrier(jnp.sum(adjoint_out.astype(jnp.float32), axis=0))
        adjoint_act = jnp.dot(adjoint_out, weight_out.T, preferred_element_type=jnp.float32)
        adjoint_pre = (adjoint_act * silu_slope(preact)).astype(jnp.bfloat16)
        grad_w_in = jnp.dot(inputs.T, adjoint_pre, preferred_element_type=jnp.float32)
        grad_b_in = lax.optimization_barrier(jnp.sum(adjoint_pre.astype(jnp.float32), axis=0))
        adjoint_in = jnp.dot(adjoint_pre, weight_in.T, preferred_element_type=jnp.float32).astype(jnp.bfloat16)
        return (place_slots(adjoint_in, adjoint_grid.shape), (grad_w_in, grad_b_in, grad_w_out, grad_b_out))

    def adjoint_step(incoming, stored):
        masked = truncation * incoming
        adjoint_source = (step_size * masked).astype(jnp.bfloat16)
        adjoint_spectra = synthesis(legendre, adjoint_source).astype(jnp.bfloat16)
        adjoint_grid = fourier_synthesis(wave_table, adjoint_spectra).astype(jnp.bfloat16)
        adjoint_cols, gradients = physics_adjoint(adjoint_grid, stored)
        back_spectra = fourier_analysis(wave_table, adjoint_cols).astype(jnp.bfloat16)
        return (damping * masked + analysis(legendre, back_spectra), gradients)

    def member_run(member_inputs):
        coeffs_zero, cotangent = member_inputs
        spectra_zero = synthesis(legendre, coeffs_zero.astype(jnp.bfloat16)).astype(jnp.bfloat16)
        grid_zero = fourier_synthesis(wave_table, spectra_zero).astype(jnp.bfloat16)
        stored_zero = physics_front(grid_zero)
        tendency_zero = physics_tendency(stored_zero[2], grid_zero.shape)
        tendency_spectra = fourier_analysis(wave_table, tendency_zero).astype(jnp.bfloat16)
        coeffs_one = truncation * (damping * coeffs_zero + step_size * analysis(legendre, tendency_spectra))
        spectra_one = synthesis(legendre, coeffs_one.astype(jnp.bfloat16)).astype(jnp.bfloat16)
        grid_one = fourier_synthesis(wave_table, spectra_one).astype(jnp.bfloat16)
        stored_one = physics_front(grid_one)
        adjoint_one, grads_later = adjoint_step(cotangent, stored_one)
        adjoint_zero, grads_earlier = adjoint_step(adjoint_one, stored_zero)
        gradients = tuple((later + earlier for later, earlier in zip(grads_later, grads_earlier)))
        return (adjoint_zero, gradients)
    grad_state, gradients = lax.map(member_run, (initial_state, final_cotangent))
    norm_scale = 1.0 / math.sqrt(MEMBERS * ACTIVE)
    return (grad_state, lax.optimization_barrier(jnp.sum(gradients[0], axis=0)) * norm_scale, lax.optimization_barrier(jnp.sum(gradients[1], axis=0)) * norm_scale, lax.optimization_barrier(jnp.sum(gradients[2], axis=0)) * norm_scale, lax.optimization_barrier(jnp.sum(gradients[3], axis=0)) * norm_scale)
```

```python
import math

import jax
import jax.numpy as jnp
from jax import lax
from jax.experimental import pallas as pl
from jax.experimental.pallas import tpu as pltpu
from jax.sharding import Mesh
from jax.sharding import PartitionSpec as P

LON = 512
CAPA = 512
WAVES = 256
F = 128
HID = 384
SPACE = 64
LATS = 4
SLOTS = 4
ROWS = LATS * SLOTS * 2
ACT_TOTAL = 131072
STEP = 0.5
SPACE_AXES = ("z", "y")
MEMBER_AXES = ("x", "core")
PLANE_AXES = ("x", "core", "y")
VMEM_LIMIT = 20 * 1024 * 1024

SMEM_SPEC = pl.BlockSpec(memory_space=pltpu.SMEM)
VMEM_SPEC = pl.BlockSpec(memory_space=pltpu.VMEM)


def kernel_params():
    return pltpu.CompilerParams(vmem_limit_bytes=VMEM_LIMIT)


def dot_last(a, b):
    return lax.dot_general(a, b, (((1,), (0,)), ((), ())), preferred_element_type=jnp.float32)


def dot_first(a, b):
    return lax.dot_general(a, b, (((0,), (0,)), ((), ())), preferred_element_type=jnp.float32)


def dot_rows(a, b):
    return lax.dot_general(a, b, (((1,), (1,)), ((), ())), preferred_element_type=jnp.float32)


def factors(wave):
    degree = wave + lax.broadcasted_iota(jnp.int32, (WAVES, F), 0)
    truncation = (degree < WAVES).astype(jnp.float32)
    degree_real = degree.astype(jnp.float32)
    damping = 1.0 / (1.0 + degree_real * (degree_real + 1.0) / (WAVES * (WAVES - 1.0)))
    both = lambda v: jnp.concatenate([v, v], axis=1)
    return both(damping), both(truncation)


def put_slot(rows, s, values):
    rows[pl.ds(2 * s, WAVES, stride=8), :] = values[:, :F]
    rows[pl.ds(2 * s + 1, WAVES, stride=8), :] = values[:, F:]


def get_slot(rows, s):
    parts = [rows[pl.ds(2 * s + p, WAVES, stride=8), :] for p in range(2)]
    return jnp.concatenate(parts, axis=1).astype(jnp.bfloat16)


def start_kernel(legendre, state, out, rows):
    for s in range(SLOTS):
        put_slot(rows, s, dot_first(legendre[s], state[s].astype(jnp.bfloat16)))
    out[...] = rows[...].astype(jnp.bfloat16).reshape(out.shape)


def cotangent_kernel(waves, legendre, state, out, rows):
    for s in range(SLOTS):
        _, truncation = factors(waves[s])
        source = (STEP * (truncation * state[s])).astype(jnp.bfloat16)
        put_slot(rows, s, dot_first(legendre[s], source))
    out[...] = rows[...].astype(jnp.bfloat16).reshape(out.shape)


def forward_home_kernel(waves, arrived, legendre, state, beside, out, taken, rows):
    taken[...] = arrived[...].reshape(taken.shape).astype(jnp.float32)
    for s in range(SLOTS):
        damping, truncation = factors(waves[s])
        tendency = dot_last(legendre[s], get_slot(taken, s))
        state_one = truncation * (damping * state[s] + STEP * tendency)
        put_slot(rows, s, dot_first(legendre[s], state_one.astype(jnp.bfloat16)))
    out[:, :ROWS, :] = rows[...].astype(jnp.bfloat16).reshape(SPACE, ROWS, F)
    out[:, ROWS:, :] = beside[...]


def adjoint_home_kernel(waves, arrived, legendre, cotangent, out, masked_out, taken, rows):
    taken[...] = arrived[...].reshape(taken.shape).astype(jnp.float32)
    for s in range(SLOTS):
        damping, truncation = factors(waves[s])
        outgoing = damping * (truncation * cotangent[s]) + dot_last(legendre[s], get_slot(taken, s))
        masked = truncation * outgoing
        masked_out[s] = masked
        put_slot(rows, s, dot_first(legendre[s], (STEP * masked).astype(jnp.bfloat16)))
    out[...] = rows[...].astype(jnp.bfloat16).reshape(out.shape)


def last_home_kernel(waves, arrived, legendre, masked, out, taken):
    taken[...] = arrived[...].reshape(taken.shape).astype(jnp.float32)
    for s in range(SLOTS):
        damping, _ = factors(waves[s])
        out[s] = damping * masked[s] + dot_last(legendre[s], get_slot(taken, s))


def forward_band_kernel(
    arrived, pick, place, weight_in, bias_in, weight_out, bias_out, out, inputs_out
):
    inputs = dot_last(pick[...], arrived[...].reshape(SPACE * ROWS, F)).astype(jnp.bfloat16)
    inputs_out[...] = inputs
    preact = dot_last(inputs, weight_in[...]) + bias_in[...]
    active = (preact * jax.nn.sigmoid(preact)).astype(jnp.bfloat16)
    tendency = (dot_last(active, weight_out[...]) + bias_out[...]).astype(jnp.bfloat16)
    out[...] = dot_last(place[...], tendency).astype(jnp.bfloat16).reshape(out.shape)


def physics_adjoint(inputs, adjoint_out, weight_in, bias_in, weight_out):
    preact = dot_last(inputs, weight_in) + bias_in
    sig = jax.nn.sigmoid(preact)
    active = (preact * sig).astype(jnp.bfloat16)
    slope = sig * (1.0 + preact * (1.0 - sig))
    adjoint_pre = (dot_rows(adjoint_out, weight_out) * slope).astype(jnp.bfloat16)
    adjoint_in = dot_rows(adjoint_pre, weight_in).astype(jnp.bfloat16)
    return active, adjoint_pre, adjoint_in


def gradients(inputs, active, adjoint_out, adjoint_pre):
    grad_in = dot_first(inputs, adjoint_pre)
    blocks = [grad_in[:, F * i : F * (i + 1)] for i in range(HID // F)]
    weights = jnp.concatenate(blocks + [dot_first(active, adjoint_out)], axis=0)
    bias_in = jnp.sum(adjoint_pre.astype(jnp.float32), axis=0, keepdims=True)
    bias_out = jnp.sum(adjoint_out.astype(jnp.float32), axis=0, keepdims=True)
    biases = [bias_in[:, F * i : F * (i + 1)] for i in range(HID // F)] + [bias_out]
    return weights, biases


def turn_band_kernel(arrived, pick, place, weight_in, bias_in, weight_out, out, grads_out):
    forward = arrived[:, :ROWS, :].reshape(SPACE * ROWS, F)
    adjoint = arrived[:, ROWS:, :].reshape(SPACE * ROWS, F)
    both = dot_last(pick[...], jnp.concatenate([forward, adjoint], axis=1)).astype(jnp.bfloat16)
    inputs, adjoint_out = both[:, :F], both[:, F:]
    active, adjoint_pre, adjoint_in = physics_adjoint(
        inputs, adjoint_out, weight_in[...], bias_in[...], weight_out[...]
    )
    out[...] = dot_last(place[...], adjoint_in).astype(jnp.bfloat16).reshape(out.shape)
    weights, biases = gradients(inputs, active, adjoint_out, adjoint_pre)
    grads_out[...] = jnp.zeros_like(grads_out)
    grads_out[:, :24, :] = weights.reshape(32, 24, F)
    for i, row in enumerate(biases):
        grads_out[i, 24:25, :] = row


def last_band_kernel(
    arrived, pick, place, inputs_ref, weight_in, bias_in, weight_out, earlier, out, grads_out, total
):
    adjoint = arrived[...].reshape(SPACE * ROWS, F)
    adjoint_out = dot_last(pick[...], adjoint).astype(jnp.bfloat16)
    inputs = inputs_ref[...]
    active, adjoint_pre, adjoint_in = physics_adjoint(
        inputs, adjoint_out, weight_in[...], bias_in[...], weight_out[...]
    )
    out[...] = dot_last(place[...], adjoint_in).astype(jnp.bfloat16).reshape(out.shape)
    weights, biases = gradients(inputs, active, adjoint_out, adjoint_pre)
    total[...] = earlier[...]
    total[:, :24, :] = earlier[:, :24, :] + weights.reshape(32, 24, F)
    for i, row in enumerate(biases):
        total[i, 24:25, :] = earlier[i, 24:25, :] + row
    grads_out[...] = total[...].astype(jnp.bfloat16)


def plane_sum_kernel(parts, out):
    total = jnp.sum(parts[...].astype(jnp.float32), axis=0, keepdims=True)
    out[...] = jnp.broadcast_to(total.astype(jnp.bfloat16), out.shape)


def unpack_kernel(whole, grad_in, grad_bias_in, grad_out, grad_bias_out):
    weights = whole[:, :24, :].reshape(768, F)
    for i in range(3):
        grad_in[:, F * i : F * (i + 1)] = weights[F * i : F * (i + 1)]
        grad_bias_in[:, F * i : F * (i + 1)] = whole[i, 24:25, :]
    grad_out[...] = weights[HID:]
    grad_bias_out[...] = whole[3, 24:25, :]


def call(kernel, outs, specs, scratch=(), name=None):
    return pl.pallas_call(
        kernel,
        out_shape=outs,
        in_specs=specs,
        out_specs=jax.tree.map(lambda _: VMEM_SPEC, outs),
        scratch_shapes=list(scratch),
        compiler_params=kernel_params(),
        name=name,
    )


def travel(block):
    return lax.all_to_all(block, SPACE_AXES, split_axis=0, concat_axis=0, tiled=True)


def fourier_table(wave_ids):
    longitude = jnp.arange(LON, dtype=jnp.int32)
    phase_index = wave_ids[:, None] * longitude[None, :] % LON
    angles = phase_index.astype(jnp.float32) * (2.0 * math.pi / LON)
    norm_scale = 1.0 / math.sqrt(WAVES)
    stacked = jnp.stack([jnp.cos(angles), -jnp.sin(angles)], axis=1) * norm_scale
    return stacked.astype(jnp.bfloat16)


def column_matrices(wave_map, column_list, column_count):
    table = fourier_table(wave_map).reshape(SPACE, 1, SLOTS * 2, LON)
    table = jnp.broadcast_to(table, (SPACE, LATS, SLOTS * 2, LON)).reshape(SPACE * ROWS, LON)
    columns = column_list[0, :CAPA]
    valid = jnp.arange(CAPA, dtype=jnp.int32) < column_count[0]
    longitude = jnp.arange(LON, dtype=jnp.int32)
    chosen = (columns % LON)[:, None] == longitude[None, :]
    chosen = (chosen & valid[:, None]).astype(jnp.bfloat16)
    row_lat = (jnp.arange(SPACE * ROWS, dtype=jnp.int32) // (SLOTS * 2)) % LATS
    slot_lat = columns // LON
    pick = jnp.einsum("cn,rn->cr", chosen, table, preferred_element_type=jnp.float32)
    pick = jnp.where(slot_lat[:, None] == row_lat[None, :], pick, 0.0).astype(jnp.bfloat16)
    place = jnp.einsum("rn,cn->rc", table, chosen, preferred_element_type=jnp.float32)
    place = jnp.where(row_lat[:, None] == slot_lat[None, :], place, 0.0).astype(jnp.bfloat16)
    return pick, place


def body(
    initial_state,
    final_cotangent,
    legendre,
    wave_map,
    column_list,
    column_count,
    weight_in,
    bias_in,
    weight_out,
    bias_out,
):
    own = lax.axis_index(SPACE_AXES) * SLOTS
    waves = lax.dynamic_slice_in_dim(wave_map, own, SLOTS)
    state, cotangent = initial_state[0], final_cotangent[0]
    bias_in, bias_out = bias_in[None], bias_out[None]
    block = jax.ShapeDtypeStruct((SPACE, ROWS, F), jnp.bfloat16)
    wide = jax.ShapeDtypeStruct((SPACE, 2 * ROWS, F), jnp.bfloat16)
    full = jax.ShapeDtypeStruct((SLOTS, WAVES, 2 * F), jnp.float32)
    grads = jax.ShapeDtypeStruct((32, 32, F), jnp.float32)
    rows = pltpu.VMEM((SPACE * ROWS, F), jnp.float32)
    V, S = VMEM_SPEC, SMEM_SPEC

    spectra_zero = call(start_kernel, block, [V, V], [rows], "state_synthesis")(legendre, state)
    band_zero = travel(spectra_zero)
    pick, place = column_matrices(wave_map, column_list, column_count)
    adjoint_two = call(cotangent_kernel, block, [S, V, V], [rows], "cotangent_synthesis")(
        waves, legendre, cotangent
    )
    tendency, inputs_zero = call(
        forward_band_kernel,
        (block, jax.ShapeDtypeStruct((CAPA, F), jnp.bfloat16)),
        [V] * 7,
        name="physics_forward",
    )(band_zero, pick, place, weight_in, bias_in, weight_out, bias_out)
    both = call(forward_home_kernel, wide, [S, V, V, V, V], [rows, rows], "state_step")(
        waves, travel(tendency), legendre, state, adjoint_two
    )
    back_two, grads_two = call(turn_band_kernel, (block, grads), [V] * 6, name="physics_turn")(
        travel(both), pick, place, weight_in, bias_in, weight_out
    )
    adjoint_one, masked_one = call(
        adjoint_home_kernel, (block, full), [S, V, V, V], [rows, rows], "adjoint_step"
    )(waves, travel(back_two), legendre, cotangent)
    back_one, grads_all = call(
        last_band_kernel,
        (block, jax.ShapeDtypeStruct((32, 32, F), jnp.bfloat16)),
        [V] * 8,
        [pltpu.VMEM((32, 32, F), jnp.float32)],
        "physics_adjoint",
    )(travel(adjoint_one), pick, place, inputs_zero, weight_in, bias_in, weight_out, grads_two)

    parts = lax.all_to_all(grads_all, PLANE_AXES, split_axis=0, concat_axis=0, tiled=True)
    copies = call(
        plane_sum_kernel, jax.ShapeDtypeStruct((16, 32, F), jnp.bfloat16), [V], name="plane_sum"
    )(parts)
    pieces = lax.all_to_all(copies, "z", split_axis=0, concat_axis=0, tiled=True)
    piece = jnp.sum(pieces.astype(jnp.float32), axis=0) * (1.0 / math.sqrt(ACT_TOTAL))
    whole = lax.all_gather(lax.all_gather(piece[None], "y", tiled=True), MEMBER_AXES, tiled=True)
    shape = lambda *dims: jax.ShapeDtypeStruct(dims, jnp.float32)
    grad_weight_in, grad_bias_in, grad_weight_out, grad_bias_out = call(
        unpack_kernel, (shape(F, HID), shape(1, HID), shape(HID, F), shape(1, F)), [V], name="unpack"
    )(whole)

    grad_state = call(last_home_kernel, full, [S, V, V, V], [rows], "last_analysis")(
        waves, travel(back_one), legendre, masked_one
    )

    return (
        grad_state[None],
        grad_weight_in,
        grad_bias_in[0],
        grad_weight_out,
        grad_bias_out[0],
    )


def solution(mesh):
    fine = Mesh(mesh.devices.reshape(4, 2, 16, 4), ("x", "core", "z", "y"))
    member, space = ("x", "core"), ("z", "y")
    return jax.shard_map(
        body,
        mesh=fine,
        in_specs=(
            P(member, space, None, None),
            P(member, space, None, None),
            P(space, None, None),
            P(),
            P(space, None),
            P(space),
            P(),
            P(),
            P(),
            P(),
        ),
        out_specs=(P(member, space, None, None), P(), P(), P(), P()),
        check_vma=False,
    )
```

```python
import math

import jax
import jax.numpy as jnp
from jax import lax
from jax.experimental import pallas as pl
from jax.experimental.pallas import tpu as pltpu
from jax.sharding import Mesh
from jax.sharding import PartitionSpec as P

LON = 512
CAPA = 512
WAVES = 256
F = 128
HID = 384
SPACE = 64
LATS = 4
SLOTS = 4
ROWS = LATS * SLOTS * 2
ACT_TOTAL = 131072
STEP = 0.5
SPACE_AXES = ("z", "y")
MEMBER_AXES = ("x", "core")
PLANE_AXES = ("x", "core", "y")
VMEM_LIMIT = 16 * 1024 * 1024

SMEM_SPEC = pl.BlockSpec(memory_space=pltpu.SMEM)
VMEM_SPEC = pl.BlockSpec(memory_space=pltpu.VMEM)


def kernel_params():
    return pltpu.CompilerParams(vmem_limit_bytes=VMEM_LIMIT)


def dot_last(a, b):
    return lax.dot_general(a, b, (((1,), (0,)), ((), ())), preferred_element_type=jnp.float32)


def dot_first(a, b):
    return lax.dot_general(a, b, (((0,), (0,)), ((), ())), preferred_element_type=jnp.float32)


def dot_rows(a, b):
    return lax.dot_general(a, b, (((1,), (1,)), ((), ())), preferred_element_type=jnp.float32)


def factors(wave):
    degree = wave + lax.broadcasted_iota(jnp.int32, (WAVES, F), 0)
    truncation = (degree < WAVES).astype(jnp.float32)
    degree_real = degree.astype(jnp.float32)
    damping = 1.0 / (1.0 + degree_real * (degree_real + 1.0) / (WAVES * (WAVES - 1.0)))
    both = lambda v: jnp.concatenate([v, v], axis=1)
    return both(damping), both(truncation)


def put_slot(rows, s, values):
    rows[pl.ds(2 * s, WAVES, stride=8), :] = values[:, :F]
    rows[pl.ds(2 * s + 1, WAVES, stride=8), :] = values[:, F:]


def get_slot(rows, s):
    parts = [rows[pl.ds(2 * s + p, WAVES, stride=8), :] for p in range(2)]
    return jnp.concatenate(parts, axis=1).astype(jnp.bfloat16)


def fetch(sources, targets, sems):
    copies = [
        [pltpu.make_async_copy(src.at[s], dst.at[s], sems.at[i, s]) for s in range(SLOTS)]
        for i, (src, dst) in enumerate(zip(sources, targets))
    ]
    for s in range(SLOTS):
        for one in copies:
            one[s].start()
    return copies


def start_kernel(legendre_hbm, state_hbm, out, rows, legendre, state, sems):
    copies = fetch((legendre_hbm, state_hbm), (legendre, state), sems)
    for s in range(SLOTS):
        for one in copies:
            one[s].wait()
        put_slot(rows, s, dot_first(legendre[s], state[s].astype(jnp.bfloat16)))
    out[...] = rows[...].astype(jnp.bfloat16).reshape(out.shape)


def cotangent_kernel(waves, legendre, state, out, rows):
    for s in range(SLOTS):
        _, truncation = factors(waves[s])
        source = (STEP * (truncation * state[s])).astype(jnp.bfloat16)
        put_slot(rows, s, dot_first(legendre[s], source))
    out[...] = rows[...].astype(jnp.bfloat16).reshape(out.shape)


def forward_home_kernel(waves, arrived, legendre, state, beside, out, taken, rows):
    taken[...] = arrived[...].reshape(taken.shape).astype(jnp.float32)
    for s in range(SLOTS):
        damping, truncation = factors(waves[s])
        tendency = dot_last(legendre[s], get_slot(taken, s))
        state_one = truncation * (damping * state[s] + STEP * tendency)
        put_slot(rows, s, dot_first(legendre[s], state_one.astype(jnp.bfloat16)))
    out[:, :ROWS, :] = rows[...].astype(jnp.bfloat16).reshape(SPACE, ROWS, F)
    out[:, ROWS:, :] = beside[...]


def adjoint_home_kernel(waves, arrived, legendre, cotangent, out, masked_out, taken, rows):
    taken[...] = arrived[...].reshape(taken.shape).astype(jnp.float32)
    for s in range(SLOTS):
        damping, truncation = factors(waves[s])
        outgoing = damping * (truncation * cotangent[s]) + dot_last(legendre[s], get_slot(taken, s))
        masked = truncation * outgoing
        masked_out[s] = masked
        put_slot(rows, s, dot_first(legendre[s], (STEP * masked).astype(jnp.bfloat16)))
    out[...] = rows[...].astype(jnp.bfloat16).reshape(out.shape)


def last_home_kernel(waves, arrived, legendre, masked, out_hbm, taken, out, sems):
    taken[...] = arrived[...].reshape(taken.shape).astype(jnp.float32)
    copies = []
    for s in range(SLOTS):
        damping, _ = factors(waves[s])
        out[s] = damping * masked[s] + dot_last(legendre[s], get_slot(taken, s))
        copies.append(pltpu.make_async_copy(out.at[s], out_hbm.at[s], sems.at[s]))
        copies[s].start()
    for copy in copies:
        copy.wait()


def forward_band_kernel(
    arrived, pick, place, weight_in, bias_in, weight_out, bias_out, out, inputs_out
):
    inputs = dot_last(pick[...], arrived[...].reshape(SPACE * ROWS, F)).astype(jnp.bfloat16)
    inputs_out[...] = inputs
    preact = dot_last(inputs, weight_in[...]) + bias_in[...]
    active = (preact * jax.nn.sigmoid(preact)).astype(jnp.bfloat16)
    tendency = (dot_last(active, weight_out[...]) + bias_out[...]).astype(jnp.bfloat16)
    out[...] = dot_last(place[...], tendency).astype(jnp.bfloat16).reshape(out.shape)


def physics_adjoint(inputs, adjoint_out, weight_in, bias_in, weight_out):
    preact = dot_last(inputs, weight_in) + bias_in
    sig = jax.nn.sigmoid(preact)
    active = (preact * sig).astype(jnp.bfloat16)
    slope = sig * (1.0 + preact * (1.0 - sig))
    adjoint_pre = (dot_rows(adjoint_out, weight_out) * slope).astype(jnp.bfloat16)
    adjoint_in = dot_rows(adjoint_pre, weight_in).astype(jnp.bfloat16)
    return active, adjoint_pre, adjoint_in


def gradients(inputs, active, adjoint_out, adjoint_pre):
    grad_in = dot_first(inputs, adjoint_pre)
    blocks = [grad_in[:, F * i : F * (i + 1)] for i in range(HID // F)]
    weights = jnp.concatenate(blocks + [dot_first(active, adjoint_out)], axis=0)
    bias_in = jnp.sum(adjoint_pre.astype(jnp.float32), axis=0, keepdims=True)
    bias_out = jnp.sum(adjoint_out.astype(jnp.float32), axis=0, keepdims=True)
    biases = [bias_in[:, F * i : F * (i + 1)] for i in range(HID // F)] + [bias_out]
    return weights, biases


def turn_band_kernel(arrived, pick, place, weight_in, bias_in, weight_out, out, grads_out):
    forward = arrived[:, :ROWS, :].reshape(SPACE * ROWS, F)
    adjoint = arrived[:, ROWS:, :].reshape(SPACE * ROWS, F)
    both = dot_last(pick[...], jnp.concatenate([forward, adjoint], axis=1)).astype(jnp.bfloat16)
    inputs, adjoint_out = both[:, :F], both[:, F:]
    active, adjoint_pre, adjoint_in = physics_adjoint(
        inputs, adjoint_out, weight_in[...], bias_in[...], weight_out[...]
    )
    out[...] = dot_last(place[...], adjoint_in).astype(jnp.bfloat16).reshape(out.shape)
    weights, biases = gradients(inputs, active, adjoint_out, adjoint_pre)
    grads_out[...] = jnp.zeros_like(grads_out)
    grads_out[:, :24, :] = weights.reshape(32, 24, F)
    for i, row in enumerate(biases):
        grads_out[i, 24:25, :] = row


def last_band_kernel(
    arrived, pick, inputs_ref, weight_in, bias_in, weight_out, earlier, adj_in_out, grads_out, total
):
    adjoint = arrived[...].reshape(SPACE * ROWS, F)
    adjoint_out = dot_last(pick[...], adjoint).astype(jnp.bfloat16)
    inputs = inputs_ref[...]
    active, adjoint_pre, adjoint_in = physics_adjoint(
        inputs, adjoint_out, weight_in[...], bias_in[...], weight_out[...]
    )
    adj_in_out[...] = adjoint_in
    weights, biases = gradients(inputs, active, adjoint_out, adjoint_pre)
    total[...] = earlier[...]
    total[:, :24, :] = earlier[:, :24, :] + weights.reshape(32, 24, F)
    for i, row in enumerate(biases):
        total[i, 24:25, :] = earlier[i, 24:25, :] + row
    grads_out[...] = total[...].astype(jnp.bfloat16)


def place_kernel(place, values, out):
    out[...] = dot_last(place[...], values[...]).astype(jnp.bfloat16).reshape(out.shape)


def plane_sum_kernel(parts, out):
    total = jnp.sum(parts[...].astype(jnp.float32), axis=0, keepdims=True)
    out[...] = jnp.broadcast_to(total.astype(jnp.bfloat16), out.shape)


def unpack_kernel(whole, grad_in, grad_bias_in, grad_out, grad_bias_out):
    weights = whole[:, :24, :].reshape(768, F)
    for i in range(3):
        grad_in[:, F * i : F * (i + 1)] = weights[F * i : F * (i + 1)]
        grad_bias_in[:, F * i : F * (i + 1)] = whole[i, 24:25, :]
    grad_out[...] = weights[HID:]
    grad_bias_out[...] = whole[3, 24:25, :]


def call(kernel, outs, specs, scratch=(), name=None, out_specs=None):
    return pl.pallas_call(
        kernel,
        out_shape=outs,
        in_specs=specs,
        out_specs=out_specs or jax.tree.map(lambda _: VMEM_SPEC, outs),
        scratch_shapes=list(scratch),
        compiler_params=kernel_params(),
        name=name,
    )


def in_hbm(x):
    return pltpu.with_memory_space_constraint(x, pltpu.HBM)


def in_vmem(x):
    return pltpu.with_memory_space_constraint(x, pltpu.VMEM)


def travel(block):
    return lax.all_to_all(block, SPACE_AXES, split_axis=0, concat_axis=0, tiled=True)


def fourier_table(wave_ids):
    longitude = jnp.arange(LON, dtype=jnp.int32)
    phase_index = wave_ids[:, None] * longitude[None, :] % LON
    angles = phase_index.astype(jnp.float32) * (2.0 * math.pi / LON)
    norm_scale = 1.0 / math.sqrt(WAVES)
    stacked = jnp.stack([jnp.cos(angles), -jnp.sin(angles)], axis=1) * norm_scale
    return stacked.astype(jnp.bfloat16)


def column_matrices(wave_map, column_list, column_count):
    table = fourier_table(wave_map).reshape(SPACE, 1, SLOTS * 2, LON)
    table = jnp.broadcast_to(table, (SPACE, LATS, SLOTS * 2, LON)).reshape(SPACE * ROWS, LON)
    columns = column_list[0, :CAPA]
    valid = jnp.arange(CAPA, dtype=jnp.int32) < column_count[0]
    longitude = jnp.arange(LON, dtype=jnp.int32)
    chosen = (columns % LON)[:, None] == longitude[None, :]
    chosen = (chosen & valid[:, None]).astype(jnp.bfloat16)
    row_lat = (jnp.arange(SPACE * ROWS, dtype=jnp.int32) // (SLOTS * 2)) % LATS
    slot_lat = columns // LON
    pick = jnp.einsum("cn,rn->cr", chosen, table, preferred_element_type=jnp.float32)
    pick = jnp.where(slot_lat[:, None] == row_lat[None, :], pick, 0.0).astype(jnp.bfloat16)
    place = jnp.einsum("rn,cn->rc", table, chosen, preferred_element_type=jnp.float32)
    place = jnp.where(row_lat[:, None] == slot_lat[None, :], place, 0.0).astype(jnp.bfloat16)
    return pick, place


def body(
    initial_state,
    final_cotangent,
    legendre,
    wave_map,
    column_list,
    column_count,
    weight_in,
    bias_in,
    weight_out,
    bias_out,
):
    own = lax.axis_index(SPACE_AXES) * SLOTS
    waves = lax.dynamic_slice_in_dim(wave_map, own, SLOTS)
    state, cotangent = initial_state[0], final_cotangent[0]
    bias_in, bias_out = bias_in[None], bias_out[None]
    block = pltpu.VMEM((SPACE, ROWS, F), jnp.bfloat16)
    narrow = pltpu.VMEM((CAPA, F), jnp.bfloat16)
    wide = pltpu.VMEM((SPACE, 2 * ROWS, F), jnp.bfloat16)
    full = jax.ShapeDtypeStruct((SLOTS, WAVES, 2 * F), jnp.float32)
    kept = pltpu.VMEM((SLOTS, WAVES, 2 * F), jnp.float32)
    grads = pltpu.VMEM((32, 32, F), jnp.float32)
    rows = pltpu.VMEM((SPACE * ROWS, F), jnp.float32)
    copied = pltpu.VMEM((SLOTS, WAVES, 2 * F), jnp.float32)
    sems = lambda *shape: pltpu.SemaphoreType.DMA(shape)
    V, S, A = VMEM_SPEC, SMEM_SPEC, pl.BlockSpec(memory_space=pltpu.HBM)

    spectra_zero = call(
        start_kernel,
        block,
        [A, A],
        [rows, pltpu.VMEM((SLOTS, WAVES, WAVES), jnp.bfloat16), copied, sems(2, SLOTS)],
        "state_synthesis",
    )(in_hbm(legendre), in_hbm(state))
    band_zero = travel(spectra_zero)
    pick, place = map(in_vmem, column_matrices(wave_map, column_list, column_count))
    adjoint_two = call(cotangent_kernel, block, [S, V, V], [rows], "cotangent_synthesis")(
        waves, legendre, cotangent
    )
    band_zero, adjoint_two = lax.optimization_barrier((band_zero, adjoint_two))
    tendency, inputs_zero = call(
        forward_band_kernel, (block, narrow), [V] * 7, name="physics_forward"
    )(band_zero, pick, place, weight_in, bias_in, weight_out, bias_out)
    both = call(forward_home_kernel, wide, [S, V, V, V, V], [rows, rows], "state_step")(
        waves, travel(tendency), legendre, state, adjoint_two
    )
    back_two, grads_two = call(turn_band_kernel, (block, grads), [V] * 6, name="physics_turn")(
        travel(both), pick, place, weight_in, bias_in, weight_out
    )
    adjoint_one, masked_one = call(
        adjoint_home_kernel, (block, kept), [S, V, V, V], [rows, rows], "adjoint_step"
    )(waves, travel(back_two), legendre, cotangent)
    adjoint_in, grads_all = call(
        last_band_kernel,
        (
            narrow,
            pltpu.VMEM((32, 32, F), jnp.bfloat16),
        ),
        [V] * 7,
        [pltpu.VMEM((32, 32, F), jnp.float32)],
        "physics_adjoint",
    )(travel(adjoint_one), pick, inputs_zero, weight_in, bias_in, weight_out, grads_two)

    parts = lax.all_to_all(grads_all, PLANE_AXES, split_axis=0, concat_axis=0, tiled=True)
    back_one = call(place_kernel, block, [V, V], name="place_adjoint")(place, adjoint_in)
    arrived = travel(back_one)
    copies = call(
        plane_sum_kernel, jax.ShapeDtypeStruct((16, 32, F), jnp.bfloat16), [V], name="plane_sum"
    )(parts)
    pieces = lax.all_to_all(copies, "z", split_axis=0, concat_axis=0, tiled=True)
    piece = jnp.sum(pieces.astype(jnp.float32), axis=0) * (1.0 / math.sqrt(ACT_TOTAL))
    whole = lax.all_gather(lax.all_gather(piece[None], "y", tiled=True), MEMBER_AXES, tiled=True)
    shape = lambda *dims: jax.ShapeDtypeStruct(dims, jnp.float32)
    grad_weight_in, grad_bias_in, grad_weight_out, grad_bias_out = call(
        unpack_kernel, (shape(F, HID), shape(1, HID), shape(HID, F), shape(1, F)), [V], name="unpack"
    )(whole)

    grad_state = call(
        last_home_kernel, full, [S, V, V, V], [rows, copied, sems(SLOTS)], "last_analysis", A
    )(waves, arrived, legendre, masked_one)

    return (
        grad_state[None],
        grad_weight_in,
        grad_bias_in[0],
        grad_weight_out,
        grad_bias_out[0],
    )


def solution(mesh):
    fine = Mesh(mesh.devices.reshape(4, 2, 16, 4), ("x", "core", "z", "y"))
    member, space = ("x", "core"), ("z", "y")
    return jax.shard_map(
        body,
        mesh=fine,
        in_specs=(
            P(member, space, None, None),
            P(member, space, None, None),
            P(space, None, None),
            P(),
            P(space, None),
            P(space),
            P(),
            P(),
            P(),
            P(),
        ),
        out_specs=(P(member, space, None, None), P(), P(), P(), P()),
        check_vma=False,
    )
```

```python
import math

import jax
import jax.numpy as jnp
from jax import lax
from jax.experimental import pallas as pl
from jax.experimental.pallas import tpu as pltpu
from jax.sharding import Mesh
from jax.sharding import PartitionSpec as P

LON = 512
CAPA = 512
WAVES = 256
F = 128
HID = 384
SPACE = 64
LATS = 4
SLOTS = 4
ROWS = LATS * SLOTS * 2
ACT_TOTAL = 131072
STEP = 0.5
SPACE_AXES = ("z", "y")
MEMBER_AXES = ("x", "core")
PLANE_AXES = ("x", "core", "y")
VMEM_LIMIT = 12 * 1024 * 1024

SMEM_SPEC = pl.BlockSpec(memory_space=pltpu.SMEM)
VMEM_SPEC = pl.BlockSpec(memory_space=pltpu.VMEM)


def kernel_params():
    return pltpu.CompilerParams(vmem_limit_bytes=VMEM_LIMIT)


def dot_last(a, b):
    return lax.dot_general(a, b, (((1,), (0,)), ((), ())), preferred_element_type=jnp.float32)


def dot_first(a, b):
    return lax.dot_general(a, b, (((0,), (0,)), ((), ())), preferred_element_type=jnp.float32)


def dot_rows(a, b):
    return lax.dot_general(a, b, (((1,), (1,)), ((), ())), preferred_element_type=jnp.float32)


def placed(pick, values, shape):
    return dot_first(values, pick).T.astype(jnp.bfloat16).reshape(shape)


def factors(wave):
    degree = wave + lax.broadcasted_iota(jnp.int32, (WAVES, F), 0)
    truncation = (degree < WAVES).astype(jnp.float32)
    degree_real = degree.astype(jnp.float32)
    damping = 1.0 / (1.0 + degree_real * (degree_real + 1.0) / (WAVES * (WAVES - 1.0)))
    both = lambda v: jnp.concatenate([v, v], axis=1)
    return both(damping), both(truncation)


def put_slot(rows, s, values):
    rows[pl.ds(2 * s, WAVES, stride=8), :] = values[:, :F]
    rows[pl.ds(2 * s + 1, WAVES, stride=8), :] = values[:, F:]


def get_slot(rows, s):
    parts = [rows[pl.ds(2 * s + p, WAVES, stride=8), :] for p in range(2)]
    return jnp.concatenate(parts, axis=1).astype(jnp.bfloat16)


def fetch(sources, targets, sems):
    copies = [
        [pltpu.make_async_copy(src.at[s], dst.at[s], sems.at[i, s]) for s in range(SLOTS)]
        for i, (src, dst) in enumerate(zip(sources, targets))
    ]
    for s in range(SLOTS):
        for one in copies:
            one[s].start()
    return copies


def start_kernel(legendre_hbm, state_hbm, out, rows, legendre, state, sems):
    copies = fetch((legendre_hbm, state_hbm), (legendre, state), sems)
    for s in range(SLOTS):
        for one in copies:
            one[s].wait()
        put_slot(rows, s, dot_first(legendre[s], state[s].astype(jnp.bfloat16)))
    out[...] = rows[...].astype(jnp.bfloat16).reshape(out.shape)


def cotangent_kernel(waves, legendre, state, out, rows):
    for s in range(SLOTS):
        _, truncation = factors(waves[s])
        source = (STEP * (truncation * state[s])).astype(jnp.bfloat16)
        put_slot(rows, s, dot_first(legendre[s], source))
    out[...] = rows[...].astype(jnp.bfloat16).reshape(out.shape)


def forward_home_kernel(waves, arrived, legendre, state, beside, out, taken, rows):
    taken[...] = arrived[...].reshape(taken.shape).astype(jnp.float32)
    for s in range(SLOTS):
        damping, truncation = factors(waves[s])
        tendency = dot_last(legendre[s], get_slot(taken, s))
        state_one = truncation * (damping * state[s] + STEP * tendency)
        put_slot(rows, s, dot_first(legendre[s], state_one.astype(jnp.bfloat16)))
    out[:, :ROWS, :] = rows[...].astype(jnp.bfloat16).reshape(SPACE, ROWS, F)
    out[:, ROWS:, :] = beside[...]


def adjoint_home_kernel(waves, arrived, legendre, cotangent, out, masked_out, taken, rows):
    taken[...] = arrived[...].reshape(taken.shape).astype(jnp.float32)
    for s in range(SLOTS):
        damping, truncation = factors(waves[s])
        outgoing = damping * (truncation * cotangent[s]) + dot_last(legendre[s], get_slot(taken, s))
        masked = truncation * outgoing
        masked_out[s] = masked
        put_slot(rows, s, dot_first(legendre[s], (STEP * masked).astype(jnp.bfloat16)))
    out[...] = rows[...].astype(jnp.bfloat16).reshape(out.shape)


def last_home_kernel(waves, arrived, legendre, masked, out_hbm, taken, out, sems):
    taken[...] = arrived[...].reshape(taken.shape).astype(jnp.float32)
    copies = []
    for s in range(SLOTS):
        damping, _ = factors(waves[s])
        out[s] = damping * masked[s] + dot_last(legendre[s], get_slot(taken, s))
        copies.append(pltpu.make_async_copy(out.at[s], out_hbm.at[s], sems.at[s]))
        copies[s].start()
    for copy in copies:
        copy.wait()


def forward_band_kernel(
    arrived, pick, weight_in, bias_in, weight_out, bias_out, out, inputs_out
):
    inputs = dot_last(pick[...], arrived[...].reshape(SPACE * ROWS, F)).astype(jnp.bfloat16)
    inputs_out[...] = inputs
    preact = dot_last(inputs, weight_in[...]) + bias_in[...]
    active = (preact * jax.nn.sigmoid(preact)).astype(jnp.bfloat16)
    tendency = (dot_last(active, weight_out[...]) + bias_out[...]).astype(jnp.bfloat16)
    out[...] = placed(pick[...], tendency, out.shape)


def physics_adjoint(inputs, adjoint_out, weight_in, bias_in, weight_out):
    preact = dot_last(inputs, weight_in) + bias_in
    sig = jax.nn.sigmoid(preact)
    active = (preact * sig).astype(jnp.bfloat16)
    slope = sig * (1.0 + preact * (1.0 - sig))
    adjoint_pre = (dot_rows(adjoint_out, weight_out) * slope).astype(jnp.bfloat16)
    adjoint_in = dot_rows(adjoint_pre, weight_in).astype(jnp.bfloat16)
    return active, adjoint_pre, adjoint_in


def gradients(inputs, active, adjoint_out, adjoint_pre):
    grad_in = dot_first(inputs, adjoint_pre)
    blocks = [grad_in[:, F * i : F * (i + 1)] for i in range(HID // F)]
    weights = jnp.concatenate(blocks + [dot_first(active, adjoint_out)], axis=0)
    bias_in = jnp.sum(adjoint_pre.astype(jnp.float32), axis=0, keepdims=True)
    bias_out = jnp.sum(adjoint_out.astype(jnp.float32), axis=0, keepdims=True)
    biases = [bias_in[:, F * i : F * (i + 1)] for i in range(HID // F)] + [bias_out]
    return weights, biases


def turn_band_kernel(arrived, pick, weight_in, bias_in, weight_out, out, grads_out):
    forward = arrived[:, :ROWS, :].reshape(SPACE * ROWS, F)
    adjoint = arrived[:, ROWS:, :].reshape(SPACE * ROWS, F)
    both = dot_last(pick[...], jnp.concatenate([forward, adjoint], axis=1)).astype(jnp.bfloat16)
    inputs, adjoint_out = both[:, :F], both[:, F:]
    active, adjoint_pre, adjoint_in = physics_adjoint(
        inputs, adjoint_out, weight_in[...], bias_in[...], weight_out[...]
    )
    out[...] = placed(pick[...], adjoint_in, out.shape)
    weights, biases = gradients(inputs, active, adjoint_out, adjoint_pre)
    grads_out[...] = jnp.zeros_like(grads_out)
    grads_out[:, :24, :] = weights.reshape(32, 24, F)
    for i, row in enumerate(biases):
        grads_out[i, 24:25, :] = row


def last_band_kernel(
    arrived, pick, inputs_ref, weight_in, bias_in, weight_out, earlier, adj_in_out, grads_out, total
):
    adjoint = arrived[...].reshape(SPACE * ROWS, F)
    adjoint_out = dot_last(pick[...], adjoint).astype(jnp.bfloat16)
    inputs = inputs_ref[...]
    active, adjoint_pre, adjoint_in = physics_adjoint(
        inputs, adjoint_out, weight_in[...], bias_in[...], weight_out[...]
    )
    adj_in_out[...] = adjoint_in
    weights, biases = gradients(inputs, active, adjoint_out, adjoint_pre)
    total[...] = earlier[...]
    total[:, :24, :] = earlier[:, :24, :] + weights.reshape(32, 24, F)
    for i, row in enumerate(biases):
        total[i, 24:25, :] = earlier[i, 24:25, :] + row
    grads_out[...] = total[...].astype(jnp.bfloat16)


def place_kernel(pick, values, out):
    out[...] = placed(pick[...], values[...], out.shape)


def plane_sum_kernel(parts, out):
    total = jnp.sum(parts[...].astype(jnp.float32), axis=0, keepdims=True)
    out[...] = jnp.broadcast_to(total.astype(jnp.bfloat16), out.shape)


def unpack_kernel(whole, grad_in, grad_bias_in, grad_out, grad_bias_out):
    weights = whole[:, :24, :].reshape(768, F)
    for i in range(3):
        grad_in[:, F * i : F * (i + 1)] = weights[F * i : F * (i + 1)]
        grad_bias_in[F * i : F * (i + 1)] = whole[i, 24, :]
    grad_out[...] = weights[HID:]
    grad_bias_out[...] = whole[3, 24, :]


def call(kernel, outs, specs, scratch=(), name=None, out_specs=None):
    return pl.pallas_call(
        kernel,
        out_shape=outs,
        in_specs=specs,
        out_specs=out_specs or jax.tree.map(lambda _: VMEM_SPEC, outs),
        scratch_shapes=list(scratch),
        compiler_params=kernel_params(),
        name=name,
    )


def in_hbm(x):
    return pltpu.with_memory_space_constraint(x, pltpu.HBM)


def in_vmem(x):
    return pltpu.with_memory_space_constraint(x, pltpu.VMEM)


def travel(block):
    return lax.all_to_all(block, SPACE_AXES, split_axis=0, concat_axis=0, tiled=True)


def fourier_table(wave_ids):
    longitude = jnp.arange(LON, dtype=jnp.int32)
    phase_index = wave_ids[:, None] * longitude[None, :] % LON
    angles = phase_index.astype(jnp.float32) * (2.0 * math.pi / LON)
    norm_scale = 1.0 / math.sqrt(WAVES)
    stacked = jnp.stack([jnp.cos(angles), -jnp.sin(angles)], axis=1) * norm_scale
    return stacked.astype(jnp.bfloat16)


def column_matrix(wave_map, column_list, column_count):
    table = fourier_table(wave_map).reshape(SPACE, 1, SLOTS * 2, LON)
    table = jnp.broadcast_to(table, (SPACE, LATS, SLOTS * 2, LON)).reshape(SPACE * ROWS, LON)
    columns = column_list[0, :CAPA]
    valid = jnp.arange(CAPA, dtype=jnp.int32) < column_count[0]
    longitude = jnp.arange(LON, dtype=jnp.int32)
    chosen = (columns % LON)[:, None] == longitude[None, :]
    chosen = (chosen & valid[:, None]).astype(jnp.bfloat16)
    row_lat = (jnp.arange(SPACE * ROWS, dtype=jnp.int32) // (SLOTS * 2)) % LATS
    slot_lat = columns // LON
    pick = jnp.einsum("cn,rn->cr", chosen, table, preferred_element_type=jnp.float32)
    pick = jnp.where(slot_lat[:, None] == row_lat[None, :], pick, 0.0).astype(jnp.bfloat16)
    return pick


def body(
    initial_state,
    final_cotangent,
    legendre,
    wave_map,
    column_list,
    column_count,
    weight_in,
    bias_in,
    weight_out,
    bias_out,
):
    own = lax.axis_index(SPACE_AXES) * SLOTS
    waves = lax.dynamic_slice_in_dim(wave_map, own, SLOTS)
    state, cotangent = initial_state[0], final_cotangent[0]
    bias_in, bias_out = bias_in[None], bias_out[None]
    block = pltpu.VMEM((SPACE, ROWS, F), jnp.bfloat16)
    narrow = pltpu.VMEM((CAPA, F), jnp.bfloat16)
    wide = pltpu.VMEM((SPACE, 2 * ROWS, F), jnp.bfloat16)
    full = jax.ShapeDtypeStruct((SLOTS, WAVES, 2 * F), jnp.float32)
    kept = pltpu.VMEM((SLOTS, WAVES, 2 * F), jnp.float32)
    grads = pltpu.VMEM((32, 32, F), jnp.float32)
    rows = pltpu.VMEM((SPACE * ROWS, F), jnp.float32)
    copied = pltpu.VMEM((SLOTS, WAVES, 2 * F), jnp.float32)
    sems = lambda *shape: pltpu.SemaphoreType.DMA(shape)
    V, S, A = VMEM_SPEC, SMEM_SPEC, pl.BlockSpec(memory_space=pltpu.HBM)

    spectra_zero = call(
        start_kernel,
        block,
        [A, A],
        [rows, pltpu.VMEM((SLOTS, WAVES, WAVES), jnp.bfloat16), copied, sems(2, SLOTS)],
        "state_synthesis",
    )(in_hbm(legendre), in_hbm(state))
    band_zero = travel(spectra_zero)
    pick = in_vmem(column_matrix(wave_map, column_list, column_count))
    adjoint_two = call(cotangent_kernel, block, [S, V, V], [rows], "cotangent_synthesis")(
        waves, legendre, cotangent
    )
    band_zero, adjoint_two = lax.optimization_barrier((band_zero, adjoint_two))
    tendency, inputs_zero = call(
        forward_band_kernel, (block, narrow), [V] * 6, name="physics_forward"
    )(band_zero, pick, weight_in, bias_in, weight_out, bias_out)
    both = call(forward_home_kernel, wide, [S, V, V, V, V], [rows, rows], "state_step")(
        waves, travel(tendency), legendre, state, adjoint_two
    )
    back_two, grads_two = call(turn_band_kernel, (block, grads), [V] * 5, name="physics_turn")(
        travel(both), pick, weight_in, bias_in, weight_out
    )
    adjoint_one, masked_one = call(
        adjoint_home_kernel, (block, kept), [S, V, V, V], [rows, rows], "adjoint_step"
    )(waves, travel(back_two), legendre, cotangent)
    adjoint_in, grads_all = call(
        last_band_kernel,
        (
            narrow,
            pltpu.VMEM((32, 32, F), jnp.bfloat16),
        ),
        [V] * 7,
        [pltpu.VMEM((32, 32, F), jnp.float32)],
        "physics_adjoint",
    )(travel(adjoint_one), pick, inputs_zero, weight_in, bias_in, weight_out, grads_two)

    parts = lax.all_to_all(grads_all, PLANE_AXES, split_axis=0, concat_axis=0, tiled=True)
    back_one = call(place_kernel, block, [V, V], name="place_adjoint")(pick, adjoint_in)
    arrived = travel(back_one)
    copies = call(
        plane_sum_kernel, jax.ShapeDtypeStruct((16, 32, F), jnp.bfloat16), [V], name="plane_sum"
    )(parts)
    pieces = lax.all_to_all(copies, "z", split_axis=0, concat_axis=0, tiled=True)
    piece = jnp.sum(pieces.astype(jnp.float32), axis=0) * (1.0 / math.sqrt(ACT_TOTAL))
    whole = lax.all_gather(lax.all_gather(piece[None], "y", tiled=True), MEMBER_AXES, tiled=True)
    shape = lambda *dims: jax.ShapeDtypeStruct(dims, jnp.float32)
    grad_weight_in, grad_bias_in, grad_weight_out, grad_bias_out = call(
        unpack_kernel, (shape(F, HID), shape(HID), shape(HID, F), shape(F)), [V], name="unpack"
    )(whole)

    grad_state = call(
        last_home_kernel, full, [S, V, V, V], [rows, copied, sems(SLOTS)], "last_analysis", A
    )(waves, arrived, legendre, masked_one)

    return (
        grad_state[None],
        grad_weight_in,
        grad_bias_in,
        grad_weight_out,
        grad_bias_out,
    )


def solution(mesh):
    fine = Mesh(mesh.devices.reshape(4, 2, 16, 4), ("x", "core", "z", "y"))
    member, space = ("x", "core"), ("z", "y")
    return jax.shard_map(
        body,
        mesh=fine,
        in_specs=(
            P(member, space, None, None),
            P(member, space, None, None),
            P(space, None, None),
            P(),
            P(space, None),
            P(space),
            P(),
            P(),
            P(),
            P(),
        ),
        out_specs=(P(member, space, None, None), P(), P(), P(), P()),
        check_vma=False,
    )
```

```python
import math

import jax
import jax.numpy as jnp
from jax import lax
from jax.experimental import pallas as pl
from jax.experimental.pallas import tpu as pltpu
from jax.sharding import Mesh
from jax.sharding import PartitionSpec as P

LON = 512
CAPA = 512
WAVES = 256
F = 128
HID = 384
SPACE = 64
LATS = 4
SLOTS = 4
ROWS = LATS * SLOTS * 2
ACT_TOTAL = 131072
STEP = 0.5
SPACE_AXES = ("z", "y")
TRAVEL_AXES = ("y", "z")
MEMBER_AXES = ("x", "core")
PLANE_AXES = ("x", "core", "y")
VMEM_LIMIT = 12 * 1024 * 1024

SMEM_SPEC = pl.BlockSpec(memory_space=pltpu.SMEM)
VMEM_SPEC = pl.BlockSpec(memory_space=pltpu.VMEM)


def kernel_params():
    return pltpu.CompilerParams(vmem_limit_bytes=VMEM_LIMIT)


def dot_last(a, b):
    return lax.dot_general(a, b, (((1,), (0,)), ((), ())), preferred_element_type=jnp.float32)


def dot_first(a, b):
    return lax.dot_general(a, b, (((0,), (0,)), ((), ())), preferred_element_type=jnp.float32)


def dot_rows(a, b):
    return lax.dot_general(a, b, (((1,), (1,)), ((), ())), preferred_element_type=jnp.float32)


def placed(pick, values, shape):
    return dot_first(values, pick).T.astype(jnp.bfloat16).reshape(shape)


def factors(wave):
    degree = wave + lax.broadcasted_iota(jnp.int32, (WAVES, F), 0)
    truncation = (degree < WAVES).astype(jnp.float32)
    degree_real = degree.astype(jnp.float32)
    damping = 1.0 / (1.0 + degree_real * (degree_real + 1.0) / (WAVES * (WAVES - 1.0)))
    both = lambda v: jnp.concatenate([v, v], axis=1)
    return both(damping), both(truncation)


def put_slot(rows, s, values):
    rows[pl.ds(2 * s, WAVES, stride=8), :] = values[:, :F]
    rows[pl.ds(2 * s + 1, WAVES, stride=8), :] = values[:, F:]


def get_slot(rows, s):
    parts = [rows[pl.ds(2 * s + p, WAVES, stride=8), :] for p in range(2)]
    return jnp.concatenate(parts, axis=1).astype(jnp.bfloat16)


def fetch(sources, targets, sems):
    copies = [
        [pltpu.make_async_copy(src.at[s], dst.at[s], sems.at[i, s]) for s in range(SLOTS)]
        for i, (src, dst) in enumerate(zip(sources, targets))
    ]
    for s in range(SLOTS):
        for one in copies:
            one[s].start()
    return copies


def send_rows(rows, out):
    values = rows[...].astype(jnp.bfloat16).reshape(16, 4, ROWS, F)
    for y in range(4):
        out[16 * y : 16 * (y + 1), :ROWS, :] = values[:, y]


def take_rows(arrived, taken):
    parts = [arrived[16 * y : 16 * (y + 1)].astype(jnp.float32) for y in range(4)]
    taken[...] = jnp.stack(parts, axis=1).reshape(taken.shape)


def start_kernel(legendre_hbm, state_hbm, out, rows, legendre, state, sems):
    copies = fetch((legendre_hbm, state_hbm), (legendre, state), sems)
    for s in range(SLOTS):
        for one in copies:
            one[s].wait()
        put_slot(rows, s, dot_first(legendre[s], state[s].astype(jnp.bfloat16)))
    send_rows(rows, out)


def cotangent_kernel(waves, legendre, state, out, rows):
    for s in range(SLOTS):
        _, truncation = factors(waves[s])
        source = (STEP * (truncation * state[s])).astype(jnp.bfloat16)
        put_slot(rows, s, dot_first(legendre[s], source))
    send_rows(rows, out)


def forward_home_kernel(waves, arrived, legendre, state, beside, out, taken, rows):
    take_rows(arrived, taken)
    for s in range(SLOTS):
        damping, truncation = factors(waves[s])
        tendency = dot_last(legendre[s], get_slot(taken, s))
        state_one = truncation * (damping * state[s] + STEP * tendency)
        put_slot(rows, s, dot_first(legendre[s], state_one.astype(jnp.bfloat16)))
    send_rows(rows, out)
    out[:, ROWS:, :] = beside[...]


def adjoint_home_kernel(waves, arrived, legendre, cotangent, out, masked_out, taken, rows):
    take_rows(arrived, taken)
    for s in range(SLOTS):
        damping, truncation = factors(waves[s])
        outgoing = damping * (truncation * cotangent[s]) + dot_last(legendre[s], get_slot(taken, s))
        masked = truncation * outgoing
        masked_out[s] = masked
        put_slot(rows, s, dot_first(legendre[s], (STEP * masked).astype(jnp.bfloat16)))
    send_rows(rows, out)


def last_home_kernel(waves, arrived, legendre, masked, out_hbm, taken, out, sems):
    take_rows(arrived, taken)
    copies = []
    for s in range(SLOTS):
        damping, _ = factors(waves[s])
        out[s] = damping * masked[s] + dot_last(legendre[s], get_slot(taken, s))
        copies.append(pltpu.make_async_copy(out.at[s], out_hbm.at[s], sems.at[s]))
        copies[s].start()
    for copy in copies:
        copy.wait()


def forward_band_kernel(
    arrived, pick, weight_in, bias_in, weight_out, bias_out, out, inputs_out
):
    inputs = dot_last(pick[...], arrived[...].reshape(SPACE * ROWS, F)).astype(jnp.bfloat16)
    inputs_out[...] = inputs
    preact = dot_last(inputs, weight_in[...]) + bias_in[...]
    active = (preact * jax.nn.sigmoid(preact)).astype(jnp.bfloat16)
    tendency = (dot_last(active, weight_out[...]) + bias_out[...]).astype(jnp.bfloat16)
    out[...] = placed(pick[...], tendency, out.shape)


def physics_adjoint(inputs, adjoint_out, weight_in, bias_in, weight_out):
    preact = dot_last(inputs, weight_in) + bias_in
    sig = jax.nn.sigmoid(preact)
    active = (preact * sig).astype(jnp.bfloat16)
    slope = sig * (1.0 + preact * (1.0 - sig))
    adjoint_pre = (dot_rows(adjoint_out, weight_out) * slope).astype(jnp.bfloat16)
    adjoint_in = dot_rows(adjoint_pre, weight_in).astype(jnp.bfloat16)
    return active, adjoint_pre, adjoint_in


def gradients(inputs, active, adjoint_out, adjoint_pre):
    grad_in = dot_first(inputs, adjoint_pre)
    blocks = [grad_in[:, F * i : F * (i + 1)] for i in range(HID // F)]
    weights = jnp.concatenate(blocks + [dot_first(active, adjoint_out)], axis=0)
    bias_in = jnp.sum(adjoint_pre.astype(jnp.float32), axis=0, keepdims=True)
    bias_out = jnp.sum(adjoint_out.astype(jnp.float32), axis=0, keepdims=True)
    biases = [bias_in[:, F * i : F * (i + 1)] for i in range(HID // F)] + [bias_out]
    return weights, biases


def turn_band_kernel(arrived, pick, weight_in, bias_in, weight_out, out, grads_out):
    forward = arrived[:, :ROWS, :].reshape(SPACE * ROWS, F)
    adjoint = arrived[:, ROWS:, :].reshape(SPACE * ROWS, F)
    both = dot_last(pick[...], jnp.concatenate([forward, adjoint], axis=1)).astype(jnp.bfloat16)
    inputs, adjoint_out = both[:, :F], both[:, F:]
    active, adjoint_pre, adjoint_in = physics_adjoint(
        inputs, adjoint_out, weight_in[...], bias_in[...], weight_out[...]
    )
    out[...] = placed(pick[...], adjoint_in, out.shape)
    weights, biases = gradients(inputs, active, adjoint_out, adjoint_pre)
    grads_out[...] = jnp.zeros_like(grads_out)
    grads_out[:, :24, :] = weights.reshape(32, 24, F)
    for i, row in enumerate(biases):
        grads_out[i, 24:25, :] = row


def last_band_kernel(
    arrived, pick, inputs_ref, weight_in, bias_in, weight_out, earlier, adj_in_out, grads_out, total
):
    adjoint = arrived[...].reshape(SPACE * ROWS, F)
    adjoint_out = dot_last(pick[...], adjoint).astype(jnp.bfloat16)
    inputs = inputs_ref[...]
    active, adjoint_pre, adjoint_in = physics_adjoint(
        inputs, adjoint_out, weight_in[...], bias_in[...], weight_out[...]
    )
    adj_in_out[...] = adjoint_in
    weights, biases = gradients(inputs, active, adjoint_out, adjoint_pre)
    total[...] = earlier[...]
    total[:, :24, :] = earlier[:, :24, :] + weights.reshape(32, 24, F)
    for i, row in enumerate(biases):
        total[i, 24:25, :] = earlier[i, 24:25, :] + row
    grads_out[...] = total[...].astype(jnp.bfloat16)


def place_kernel(pick, values, out):
    out[...] = placed(pick[...], values[...], out.shape)


def plane_sum_kernel(parts, out):
    total = jnp.sum(parts[...].astype(jnp.float32), axis=0, keepdims=True)
    out[...] = jnp.broadcast_to(total.astype(jnp.bfloat16), out.shape)


def unpack_kernel(whole, grad_in, grad_bias_in, grad_out, grad_bias_out):
    weights = whole[:, :24, :].reshape(768, F)
    for i in range(3):
        grad_in[:, F * i : F * (i + 1)] = weights[F * i : F * (i + 1)]
        grad_bias_in[F * i : F * (i + 1)] = whole[i, 24, :]
    grad_out[...] = weights[HID:]
    grad_bias_out[...] = whole[3, 24, :]


def call(kernel, outs, specs, scratch=(), name=None, out_specs=None):
    return pl.pallas_call(
        kernel,
        out_shape=outs,
        in_specs=specs,
        out_specs=out_specs or jax.tree.map(lambda _: VMEM_SPEC, outs),
        scratch_shapes=list(scratch),
        compiler_params=kernel_params(),
        name=name,
    )


def in_hbm(x):
    return pltpu.with_memory_space_constraint(x, pltpu.HBM)


def in_vmem(x):
    return pltpu.with_memory_space_constraint(x, pltpu.VMEM)


def travel(block):
    return lax.all_to_all(block, TRAVEL_AXES, split_axis=0, concat_axis=0, tiled=True)


def fourier_table(wave_ids):
    longitude = jnp.arange(LON, dtype=jnp.int32)
    phase_index = wave_ids[:, None] * longitude[None, :] % LON
    angles = phase_index.astype(jnp.float32) * (2.0 * math.pi / LON)
    norm_scale = 1.0 / math.sqrt(WAVES)
    stacked = jnp.stack([jnp.cos(angles), -jnp.sin(angles)], axis=1) * norm_scale
    return stacked.astype(jnp.bfloat16)


def column_matrix(wave_map, column_list, column_count):
    order = wave_map.reshape(16, 4, SLOTS).transpose(1, 0, 2).reshape(-1)
    table = fourier_table(order).reshape(SPACE, 1, SLOTS * 2, LON)
    table = jnp.broadcast_to(table, (SPACE, LATS, SLOTS * 2, LON)).reshape(SPACE * ROWS, LON)
    columns = column_list[0, :CAPA]
    valid = jnp.arange(CAPA, dtype=jnp.int32) < column_count[0]
    longitude = jnp.arange(LON, dtype=jnp.int32)
    chosen = (columns % LON)[:, None] == longitude[None, :]
    chosen = (chosen & valid[:, None]).astype(jnp.bfloat16)
    row_lat = (jnp.arange(SPACE * ROWS, dtype=jnp.int32) // (SLOTS * 2)) % LATS
    slot_lat = columns // LON
    pick = jnp.einsum("cn,rn->cr", chosen, table, preferred_element_type=jnp.float32)
    pick = jnp.where(slot_lat[:, None] == row_lat[None, :], pick, 0.0).astype(jnp.bfloat16)
    return pick


def body(
    initial_state,
    final_cotangent,
    legendre,
    wave_map,
    column_list,
    column_count,
    weight_in,
    bias_in,
    weight_out,
    bias_out,
):
    own = lax.axis_index(SPACE_AXES) * SLOTS
    waves = lax.dynamic_slice_in_dim(wave_map, own, SLOTS)
    state, cotangent = initial_state[0], final_cotangent[0]
    bias_in, bias_out = bias_in[None], bias_out[None]
    block = pltpu.VMEM((SPACE, ROWS, F), jnp.bfloat16)
    narrow = pltpu.VMEM((CAPA, F), jnp.bfloat16)
    wide = pltpu.VMEM((SPACE, 2 * ROWS, F), jnp.bfloat16)
    full = jax.ShapeDtypeStruct((SLOTS, WAVES, 2 * F), jnp.float32)
    kept = pltpu.VMEM((SLOTS, WAVES, 2 * F), jnp.float32)
    grads = pltpu.VMEM((32, 32, F), jnp.float32)
    rows = pltpu.VMEM((SPACE * ROWS, F), jnp.float32)
    copied = pltpu.VMEM((SLOTS, WAVES, 2 * F), jnp.float32)
    sems = lambda *shape: pltpu.SemaphoreType.DMA(shape)
    V, S, A = VMEM_SPEC, SMEM_SPEC, pl.BlockSpec(memory_space=pltpu.HBM)

    spectra_zero = call(
        start_kernel,
        block,
        [A, A],
        [rows, pltpu.VMEM((SLOTS, WAVES, WAVES), jnp.bfloat16), copied, sems(2, SLOTS)],
        "state_synthesis",
    )(in_hbm(legendre), in_hbm(state))
    band_zero = travel(spectra_zero)
    pick = in_vmem(column_matrix(wave_map, column_list, column_count))
    adjoint_two = call(cotangent_kernel, block, [S, V, V], [rows], "cotangent_synthesis")(
        waves, legendre, cotangent
    )
    band_zero, adjoint_two = lax.optimization_barrier((band_zero, adjoint_two))
    tendency, inputs_zero = call(
        forward_band_kernel, (block, narrow), [V] * 6, name="physics_forward"
    )(band_zero, pick, weight_in, bias_in, weight_out, bias_out)
    both = call(forward_home_kernel, wide, [S, V, V, V, V], [rows, rows], "state_step")(
        waves, travel(tendency), legendre, state, adjoint_two
    )
    back_two, grads_two = call(turn_band_kernel, (block, grads), [V] * 5, name="physics_turn")(
        travel(both), pick, weight_in, bias_in, weight_out
    )
    adjoint_one, masked_one = call(
        adjoint_home_kernel, (block, kept), [S, V, V, V], [rows, rows], "adjoint_step"
    )(waves, travel(back_two), legendre, cotangent)
    adjoint_in, grads_all = call(
        last_band_kernel,
        (
            narrow,
            pltpu.VMEM((32, 32, F), jnp.bfloat16),
        ),
        [V] * 7,
        [pltpu.VMEM((32, 32, F), jnp.float32)],
        "physics_adjoint",
    )(travel(adjoint_one), pick, inputs_zero, weight_in, bias_in, weight_out, grads_two)

    parts = lax.all_to_all(grads_all, PLANE_AXES, split_axis=0, concat_axis=0, tiled=True)
    back_one = call(place_kernel, block, [V, V], name="place_adjoint")(pick, adjoint_in)
    arrived = travel(back_one)
    copies = call(
        plane_sum_kernel, jax.ShapeDtypeStruct((16, 32, F), jnp.bfloat16), [V], name="plane_sum"
    )(parts)
    pieces = lax.all_to_all(copies, "z", split_axis=0, concat_axis=0, tiled=True)
    piece = jnp.sum(pieces.astype(jnp.float32), axis=0) * (1.0 / math.sqrt(ACT_TOTAL))
    whole = lax.all_gather(lax.all_gather(piece[None], "y", tiled=True), MEMBER_AXES, tiled=True)
    shape = lambda *dims: jax.ShapeDtypeStruct(dims, jnp.float32)
    grad_weight_in, grad_bias_in, grad_weight_out, grad_bias_out = call(
        unpack_kernel, (shape(F, HID), shape(HID), shape(HID, F), shape(F)), [V], name="unpack"
    )(whole)

    grad_state = call(
        last_home_kernel, full, [S, V, V, V], [rows, copied, sems(SLOTS)], "last_analysis", A
    )(waves, arrived, legendre, masked_one)

    return (
        grad_state[None],
        grad_weight_in,
        grad_bias_in,
        grad_weight_out,
        grad_bias_out,
    )


def solution(mesh):
    fine = Mesh(mesh.devices.reshape(4, 2, 16, 4), ("x", "core", "z", "y"))
    member, space = ("x", "core"), ("z", "y")
    return jax.shard_map(
        body,
        mesh=fine,
        in_specs=(
            P(member, space, None, None),
            P(member, space, None, None),
            P(space, None, None),
            P(),
            P(space, None),
            P(space),
            P(),
            P(),
            P(),
            P(),
        ),
        out_specs=(P(member, space, None, None), P(), P(), P(), P()),
        check_vma=False,
    )
```

```python
import math

import jax
import jax.numpy as jnp
from jax import lax
from jax.experimental import pallas as pl
from jax.experimental.pallas import tpu as pltpu
from jax.sharding import Mesh
from jax.sharding import PartitionSpec as P

LON = 512
CAPA = 512
WAVES = 256
F = 128
HID = 384
SPACE = 64
LATS = 4
SLOTS = 4
ROWS = LATS * SLOTS * 2
ACT_TOTAL = 131072
STEP = 0.5
SPACE_AXES = ("z", "y")
MEMBER_AXES = ("x", "core")
PLANE_AXES = ("x", "core", "y")
VMEM_LIMIT = 12 * 1024 * 1024

SMEM_SPEC = pl.BlockSpec(memory_space=pltpu.SMEM)
VMEM_SPEC = pl.BlockSpec(memory_space=pltpu.VMEM)


def kernel_params():
    return pltpu.CompilerParams(vmem_limit_bytes=VMEM_LIMIT)


def dot_last(a, b):
    return lax.dot_general(a, b, (((1,), (0,)), ((), ())), preferred_element_type=jnp.float32)


def dot_first(a, b):
    return lax.dot_general(a, b, (((0,), (0,)), ((), ())), preferred_element_type=jnp.float32)


def dot_rows(a, b):
    return lax.dot_general(a, b, (((1,), (1,)), ((), ())), preferred_element_type=jnp.float32)


def placed(pick, values, shape):
    return dot_first(values, pick).T.astype(jnp.bfloat16).reshape(shape)


def factors(wave):
    degree = wave + lax.broadcasted_iota(jnp.int32, (WAVES, F), 0)
    truncation = (degree < WAVES).astype(jnp.float32)
    degree_real = degree.astype(jnp.float32)
    damping = 1.0 / (1.0 + degree_real * (degree_real + 1.0) / (WAVES * (WAVES - 1.0)))
    both = lambda v: jnp.concatenate([v, v], axis=1)
    return both(damping), both(truncation)


def put_slot(rows, s, values):
    rows[pl.ds(2 * s, WAVES, stride=8), :] = values[:, :F]
    rows[pl.ds(2 * s + 1, WAVES, stride=8), :] = values[:, F:]


def get_slot(rows, s):
    parts = [rows[pl.ds(2 * s + p, WAVES, stride=8), :] for p in range(2)]
    return jnp.concatenate(parts, axis=1).astype(jnp.bfloat16)


def fetch(sources, targets, sems):
    copies = [
        [pltpu.make_async_copy(src.at[s], dst.at[s], sems.at[i, s]) for s in range(SLOTS)]
        for i, (src, dst) in enumerate(zip(sources, targets))
    ]
    for s in range(SLOTS):
        for one in copies:
            one[s].start()
    return copies


def start_kernel(legendre_hbm, state_hbm, out, rows, legendre, state, sems):
    copies = fetch((legendre_hbm, state_hbm), (legendre, state), sems)
    for s in range(SLOTS):
        for one in copies:
            one[s].wait()
        put_slot(rows, s, dot_first(legendre[s], state[s].astype(jnp.bfloat16)))
    out[...] = rows[...].astype(jnp.bfloat16).reshape(out.shape)


def cotangent_kernel(waves, legendre, state, out, rows):
    for s in range(SLOTS):
        _, truncation = factors(waves[s])
        source = (STEP * (truncation * state[s])).astype(jnp.bfloat16)
        put_slot(rows, s, dot_first(legendre[s], source))
    out[...] = rows[...].astype(jnp.bfloat16).reshape(out.shape)


def forward_home_kernel(waves, arrived, legendre, state, beside, out, taken, rows):
    taken[...] = arrived[...].reshape(taken.shape).astype(jnp.float32)
    for s in range(SLOTS):
        damping, truncation = factors(waves[s])
        tendency = dot_last(legendre[s], get_slot(taken, s))
        state_one = truncation * (damping * state[s] + STEP * tendency)
        put_slot(rows, s, dot_first(legendre[s], state_one.astype(jnp.bfloat16)))
    out[:, :ROWS, :] = rows[...].astype(jnp.bfloat16).reshape(SPACE, ROWS, F)
    out[:, ROWS:, :] = beside[...]


def adjoint_home_kernel(
    waves, arrived, legendre, cotangent, out, masked_hbm, taken, rows, masked, sems
):
    taken[...] = arrived[...].reshape(taken.shape).astype(jnp.float32)
    copies = []
    for s in range(SLOTS):
        damping, truncation = factors(waves[s])
        outgoing = damping * (truncation * cotangent[s]) + dot_last(legendre[s], get_slot(taken, s))
        masked[s] = truncation * outgoing
        copies.append(pltpu.make_async_copy(masked.at[s], masked_hbm.at[s], sems.at[s]))
        copies[s].start()
    for s in range(SLOTS):
        put_slot(rows, s, dot_first(legendre[s], (STEP * masked[s]).astype(jnp.bfloat16)))
    out[...] = rows[...].astype(jnp.bfloat16).reshape(out.shape)
    for copy in copies:
        copy.wait()


def last_home_kernel(waves, arrived, legendre, masked, out_hbm, taken, out, sems):
    taken[...] = arrived[...].reshape(taken.shape).astype(jnp.float32)
    copies = []
    for s in range(SLOTS):
        damping, _ = factors(waves[s])
        out[s] = damping * masked[s] + dot_last(legendre[s], get_slot(taken, s))
        copies.append(pltpu.make_async_copy(out.at[s], out_hbm.at[s], sems.at[s]))
        copies[s].start()
    for copy in copies:
        copy.wait()


def forward_band_kernel(
    arrived, pick, weight_in, bias_in, weight_out, bias_out, out, inputs_out
):
    inputs = dot_last(pick[...], arrived[...].reshape(SPACE * ROWS, F)).astype(jnp.bfloat16)
    inputs_out[...] = inputs
    preact = dot_last(inputs, weight_in[...]) + bias_in[...]
    active = (preact * jax.nn.sigmoid(preact)).astype(jnp.bfloat16)
    tendency = (dot_last(active, weight_out[...]) + bias_out[...]).astype(jnp.bfloat16)
    out[...] = placed(pick[...], tendency, out.shape)


def physics_adjoint(inputs, adjoint_out, weight_in, bias_in, weight_out):
    preact = dot_last(inputs, weight_in) + bias_in
    sig = jax.nn.sigmoid(preact)
    active = (preact * sig).astype(jnp.bfloat16)
    slope = sig * (1.0 + preact * (1.0 - sig))
    adjoint_pre = (dot_rows(adjoint_out, weight_out) * slope).astype(jnp.bfloat16)
    adjoint_in = dot_rows(adjoint_pre, weight_in).astype(jnp.bfloat16)
    return active, adjoint_pre, adjoint_in


def gradients(inputs, active, adjoint_out, adjoint_pre):
    grad_in = dot_first(inputs, adjoint_pre)
    blocks = [grad_in[:, F * i : F * (i + 1)] for i in range(HID // F)]
    weights = jnp.concatenate(blocks + [dot_first(active, adjoint_out)], axis=0)
    bias_in = jnp.sum(adjoint_pre.astype(jnp.float32), axis=0, keepdims=True)
    bias_out = jnp.sum(adjoint_out.astype(jnp.float32), axis=0, keepdims=True)
    biases = [bias_in[:, F * i : F * (i + 1)] for i in range(HID // F)] + [bias_out]
    return weights, biases


def turn_band_kernel(arrived, pick, weight_in, bias_in, weight_out, out, grads_out):
    forward = arrived[:, :ROWS, :].reshape(SPACE * ROWS, F)
    adjoint = arrived[:, ROWS:, :].reshape(SPACE * ROWS, F)
    both = dot_last(pick[...], jnp.concatenate([forward, adjoint], axis=1)).astype(jnp.bfloat16)
    inputs, adjoint_out = both[:, :F], both[:, F:]
    active, adjoint_pre, adjoint_in = physics_adjoint(
        inputs, adjoint_out, weight_in[...], bias_in[...], weight_out[...]
    )
    out[...] = placed(pick[...], adjoint_in, out.shape)
    weights, biases = gradients(inputs, active, adjoint_out, adjoint_pre)
    grads_out[...] = jnp.zeros_like(grads_out)
    grads_out[:, :24, :] = weights.reshape(32, 24, F)
    for i, row in enumerate(biases):
        grads_out[i, 24:25, :] = row


def last_band_kernel(
    arrived, pick, inputs_ref, weight_in, bias_in, weight_out, earlier, adj_in_out, grads_out, total
):
    adjoint = arrived[...].reshape(SPACE * ROWS, F)
    adjoint_out = dot_last(pick[...], adjoint).astype(jnp.bfloat16)
    inputs = inputs_ref[...]
    active, adjoint_pre, adjoint_in = physics_adjoint(
        inputs, adjoint_out, weight_in[...], bias_in[...], weight_out[...]
    )
    adj_in_out[...] = adjoint_in
    weights, biases = gradients(inputs, active, adjoint_out, adjoint_pre)
    total[...] = earlier[...]
    total[:, :24, :] = earlier[:, :24, :] + weights.reshape(32, 24, F)
    for i, row in enumerate(biases):
        total[i, 24:25, :] = earlier[i, 24:25, :] + row
    grads_out[...] = total[...].astype(jnp.bfloat16)


def place_kernel(pick, values, out):
    out[...] = placed(pick[...], values[...], out.shape)


def plane_sum_kernel(parts, out):
    total = jnp.sum(parts[...].astype(jnp.float32), axis=0, keepdims=True)
    out[...] = jnp.broadcast_to(total.astype(jnp.bfloat16), out.shape)


def unpack_kernel(whole, grad_in, grad_bias_in, grad_out, grad_bias_out):
    weights = whole[:, :24, :].reshape(768, F)
    for i in range(3):
        grad_in[:, F * i : F * (i + 1)] = weights[F * i : F * (i + 1)]
        grad_bias_in[F * i : F * (i + 1)] = whole[i, 24, :]
    grad_out[...] = weights[HID:]
    grad_bias_out[...] = whole[3, 24, :]


def call(kernel, outs, specs, scratch=(), name=None, out_specs=None):
    return pl.pallas_call(
        kernel,
        out_shape=outs,
        in_specs=specs,
        out_specs=out_specs or jax.tree.map(lambda _: VMEM_SPEC, outs),
        scratch_shapes=list(scratch),
        compiler_params=kernel_params(),
        name=name,
    )


def in_hbm(x):
    return pltpu.with_memory_space_constraint(x, pltpu.HBM)


def in_vmem(x):
    return pltpu.with_memory_space_constraint(x, pltpu.VMEM)


def travel(block):
    return lax.all_to_all(block, SPACE_AXES, split_axis=0, concat_axis=0, tiled=True)


def fourier_table(wave_ids):
    longitude = jnp.arange(LON, dtype=jnp.int32)
    phase_index = wave_ids[:, None] * longitude[None, :] % LON
    angles = phase_index.astype(jnp.float32) * (2.0 * math.pi / LON)
    norm_scale = 1.0 / math.sqrt(WAVES)
    stacked = jnp.stack([jnp.cos(angles), -jnp.sin(angles)], axis=1) * norm_scale
    return stacked.astype(jnp.bfloat16)


def column_matrix(wave_map, column_list, column_count):
    table = fourier_table(wave_map).reshape(SPACE, 1, SLOTS * 2, LON)
    table = jnp.broadcast_to(table, (SPACE, LATS, SLOTS * 2, LON)).reshape(SPACE * ROWS, LON)
    columns = column_list[0, :CAPA]
    valid = jnp.arange(CAPA, dtype=jnp.int32) < column_count[0]
    longitude = jnp.arange(LON, dtype=jnp.int32)
    chosen = (columns % LON)[:, None] == longitude[None, :]
    chosen = (chosen & valid[:, None]).astype(jnp.bfloat16)
    row_lat = (jnp.arange(SPACE * ROWS, dtype=jnp.int32) // (SLOTS * 2)) % LATS
    slot_lat = columns // LON
    pick = jnp.einsum("cn,rn->cr", chosen, table, preferred_element_type=jnp.float32)
    pick = jnp.where(slot_lat[:, None] == row_lat[None, :], pick, 0.0).astype(jnp.bfloat16)
    return pick


def body(
    initial_state,
    final_cotangent,
    legendre,
    wave_map,
    column_list,
    column_count,
    weight_in,
    bias_in,
    weight_out,
    bias_out,
):
    own = lax.axis_index(SPACE_AXES) * SLOTS
    waves = lax.dynamic_slice_in_dim(wave_map, own, SLOTS)
    state, cotangent = initial_state[0], final_cotangent[0]
    bias_in, bias_out = bias_in[None], bias_out[None]
    block = pltpu.VMEM((SPACE, ROWS, F), jnp.bfloat16)
    narrow = pltpu.VMEM((CAPA, F), jnp.bfloat16)
    wide = pltpu.VMEM((SPACE, 2 * ROWS, F), jnp.bfloat16)
    full = jax.ShapeDtypeStruct((SLOTS, WAVES, 2 * F), jnp.float32)
    grads = pltpu.VMEM((32, 32, F), jnp.float32)
    rows = pltpu.VMEM((SPACE * ROWS, F), jnp.float32)
    copied = pltpu.VMEM((SLOTS, WAVES, 2 * F), jnp.float32)
    sems = lambda *shape: pltpu.SemaphoreType.DMA(shape)
    V, S, A = VMEM_SPEC, SMEM_SPEC, pl.BlockSpec(memory_space=pltpu.HBM)

    spectra_zero = call(
        start_kernel,
        block,
        [A, A],
        [rows, pltpu.VMEM((SLOTS, WAVES, WAVES), jnp.bfloat16), copied, sems(2, SLOTS)],
        "state_synthesis",
    )(in_hbm(legendre), in_hbm(state))
    band_zero = travel(spectra_zero)
    pick = in_vmem(column_matrix(wave_map, column_list, column_count))
    adjoint_two = call(cotangent_kernel, block, [S, V, V], [rows], "cotangent_synthesis")(
        waves, legendre, cotangent
    )
    band_zero, adjoint_two = lax.optimization_barrier((band_zero, adjoint_two))
    tendency, inputs_zero = call(
        forward_band_kernel, (block, narrow), [V] * 6, name="physics_forward"
    )(band_zero, pick, weight_in, bias_in, weight_out, bias_out)
    both = call(forward_home_kernel, wide, [S, V, V, V, V], [rows, rows], "state_step")(
        waves, travel(tendency), legendre, state, adjoint_two
    )
    back_two, grads_two = call(turn_band_kernel, (block, grads), [V] * 5, name="physics_turn")(
        travel(both), pick, weight_in, bias_in, weight_out
    )
    adjoint_one, masked_one = call(
        adjoint_home_kernel,
        (block, pltpu.HBM((SLOTS, WAVES, 2 * F), jnp.float32)),
        [S, V, V, V],
        [rows, rows, copied, sems(SLOTS)],
        "adjoint_step",
        (V, A),
    )(waves, travel(back_two), legendre, cotangent)
    adjoint_in, grads_all = call(
        last_band_kernel,
        (
            narrow,
            pltpu.VMEM((32, 32, F), jnp.bfloat16),
        ),
        [V] * 7,
        [pltpu.VMEM((32, 32, F), jnp.float32)],
        "physics_adjoint",
    )(travel(adjoint_one), pick, inputs_zero, weight_in, bias_in, weight_out, grads_two)

    parts = lax.all_to_all(grads_all, PLANE_AXES, split_axis=0, concat_axis=0, tiled=True)
    back_one = call(place_kernel, block, [V, V], name="place_adjoint")(pick, adjoint_in)
    arrived = travel(back_one)
    copies = call(
        plane_sum_kernel, jax.ShapeDtypeStruct((16, 32, F), jnp.bfloat16), [V], name="plane_sum"
    )(parts)
    pieces = lax.all_to_all(copies, "z", split_axis=0, concat_axis=0, tiled=True)
    piece = jnp.sum(pieces.astype(jnp.float32), axis=0) * (1.0 / math.sqrt(ACT_TOTAL))
    whole = lax.all_gather(lax.all_gather(piece[None], "y", tiled=True), MEMBER_AXES, tiled=True)
    shape = lambda *dims: jax.ShapeDtypeStruct(dims, jnp.float32)
    grad_weight_in, grad_bias_in, grad_weight_out, grad_bias_out = call(
        unpack_kernel, (shape(F, HID), shape(HID), shape(HID, F), shape(F)), [V], name="unpack"
    )(whole)

    grad_state = call(
        last_home_kernel, full, [S, V, V, V], [rows, copied, sems(SLOTS)], "last_analysis", A
    )(waves, arrived, legendre, masked_one)

    return (
        grad_state[None],
        grad_weight_in,
        grad_bias_in,
        grad_weight_out,
        grad_bias_out,
    )


def solution(mesh):
    fine = Mesh(mesh.devices.reshape(4, 2, 16, 4), ("x", "core", "z", "y"))
    member, space = ("x", "core"), ("z", "y")
    return jax.shard_map(
        body,
        mesh=fine,
        in_specs=(
            P(member, space, None, None),
            P(member, space, None, None),
            P(space, None, None),
            P(),
            P(space, None),
            P(space),
            P(),
            P(),
            P(),
            P(),
        ),
        out_specs=(P(member, space, None, None), P(), P(), P(), P()),
        check_vma=False,
    )
```
